128 devices in a mesh: segment: 4 (over z), blk: 32 (over y, x, core).
Axes of the slice: x: 4, y: 4, z: 4, core: 2. Of those that a mesh axis runs over, the one named last changes fastest.
Arguments:
- tokens: bfloat16 [256, 16384], P(None, 'blk'), may hold values from -6 to 6
- cotangent: bfloat16 [256, 16384], P(None, 'blk'), may hold values from -6 to 6
- first_factor: bfloat16 [4, 64, 256, 256], P('segment', 'blk'), may hold values from -0.375 to 0.375
- second_factor: bfloat16 [4, 64, 256, 1024], P('segment', 'blk'), may hold values from -0.375 to 0.375
- third_factor: bfloat16 [4, 64, 1024, 1024], P('segment', 'blk'), may hold values from -0.1875 to 0.1875
- fourth_factor: bfloat16 [4, 64, 1024, 256], P('segment', 'blk'), may hold values from -0.1875 to 0.1875
Outputs:
- segment_outputs: bfloat16 [4, 256, 16384], P('segment', None, 'blk')
- input_grads: bfloat16 [4, 256, 16384], P('segment', None, 'blk')
- first_grad: bfloat16 [4, 64, 256, 256], P('segment', 'blk')
- second_grad: bfloat16 [4, 64, 256, 1024], P('segment', 'blk')
- third_grad: bfloat16 [4, 64, 1024, 1024], P('segment', 'blk')
- fourth_grad: bfloat16 [4, 64, 1024, 256], P('segment', 'blk')
The draws below stay inside these ranges and needn't reach their ends.
All inputs are finite; a program needn't handle non-finite values.
Results may differ from the reference program's by a relative error of at most 0.035.
Values may be sent and summed in bfloat16 or wider, within the bound.
No kernel may reach another device: no remote copies, remote signals or barrier semaphores. Data moves between devices by JAX's collectives and lax.ppermute only.
A program may use at most 128 MiB of HBM per device.

```python
import jax
import jax.numpy as jnp

D = 16384
BLOCKS = 64
BW = 256
HB = 1024
TOKENS = 256
LAYERS = 4


def steps_of(own_key, shape, split, low, largest):
    def one(dim, shards_of):
        steps = jax.random.uniform(jax.random.fold_in(jax.random.fold_in(own_key, 6), dim), (shards_of,), jnp.float32, low / len(split), largest / len(split))
        return jnp.repeat(jnp.exp(steps), shape[dim] // shards_of).reshape((-1,) + (1,) * (len(shape) - dim - 1))

    factor_of = one(*split[0])
    for cut in split[1:]:
        factor_of = factor_of * one(*cut)
    return factor_of


def centred(key, extent, scale, reach, pieces=(), held_as=jnp.bfloat16):
    entries = scale * jax.random.normal(key, extent, jnp.float32)
    if pieces:
        entries = entries * steps_of(key, extent, pieces, -0.22, 0.18)
    return jnp.clip(entries, -reach, reach).astype(held_as)


def setup_inputs(seed: int = 0) -> dict:
    arg_keys = jax.random.split(jax.random.key(seed), 7)
    tokens = centred(arg_keys[0], (TOKENS, D), 1.0, 6.0, ((1, 32),))
    cotangent = centred(arg_keys[1], (TOKENS, D), 1.0, 6.0, ((1, 32),))
    first_factor = centred(arg_keys[2], (LAYERS, BLOCKS, BW, BW), BW ** -0.5, 0.375, ((0, 4), (1, 32)))
    second_factor = centred(arg_keys[3], (LAYERS, BLOCKS, BW, HB), BW ** -0.5, 0.375, ((0, 4), (1, 32)))
    third_factor = centred(arg_keys[4], (LAYERS, BLOCKS, HB, HB), HB ** -0.5, 0.1875, ((0, 4), (1, 32)))
    fourth_factor = centred(arg_keys[5], (LAYERS, BLOCKS, HB, BW), HB ** -0.5, 0.1875, ((0, 4), (1, 32)))
    return dict(tokens=tokens, cotangent=cotangent, first_factor=first_factor, second_factor=second_factor, third_factor=third_factor, fourth_factor=fourth_factor)


def layer_forward(inputs, first, second, third, fourth):
    count = inputs.shape[0]
    inner_first = BW // BLOCKS
    inner_second = HB // BLOCKS
    blocked = inputs.reshape(count, BLOCKS, BW).astype(jnp.float32)
    mixed = jnp.einsum('tki,kij->tkj', blocked, first.astype(jnp.float32)).astype(jnp.bfloat16)
    grouped = mixed.reshape(count, BLOCKS, BLOCKS, inner_first)
    second_view = second.reshape(BLOCKS, BLOCKS, inner_first, HB)
    pre = jnp.einsum('tkgc,gkcm->tgm', grouped.astype(jnp.float32), second_view.astype(jnp.float32)).astype(jnp.bfloat16)
    activated = jax.nn.gelu(pre.astype(jnp.float32)).astype(jnp.bfloat16)
    spread = jnp.einsum('tgm,gmn->tgn', activated.astype(jnp.float32), third.astype(jnp.float32)).astype(jnp.bfloat16)
    spread_view = spread.reshape(count, BLOCKS, BLOCKS, inner_second)
    fourth_view = fourth.reshape(BLOCKS, BLOCKS, inner_second, BW)
    branch = jnp.einsum('tgkc,kgco->tko', spread_view.astype(jnp.float32), fourth_view.astype(jnp.float32))
    output = (inputs.astype(jnp.float32) + branch.reshape(count, D)).astype(jnp.bfloat16)
    return (output, (grouped, pre, activated, spread_view))

def layer_backward(inputs, upstream, saved, first, second, third, fourth):
    count = inputs.shape[0]
    inner_first = BW // BLOCKS
    inner_second = HB // BLOCKS
    grouped, pre, activated, spread_view = saved
    second_view = second.reshape(BLOCKS, BLOCKS, inner_first, HB)
    fourth_view = fourth.reshape(BLOCKS, BLOCKS, inner_second, BW)
    upper = upstream.reshape(count, BLOCKS, BW).astype(jnp.float32)
    grad_fourth = jnp.einsum('tgkc,tko->kgco', spread_view.astype(jnp.float32), upper).reshape(BLOCKS, HB, BW)
    grad_spread = jnp.einsum('tko,kgco->tgkc', upper, fourth_view.astype(jnp.float32)).astype(jnp.bfloat16)
    grad_spread = grad_spread.reshape(count, BLOCKS, HB).astype(jnp.float32)
    grad_third = jnp.einsum('tgm,tgn->gmn', activated.astype(jnp.float32), grad_spread)
    grad_act = jnp.einsum('tgn,gmn->tgm', grad_spread, third.astype(jnp.float32))
    unused, gelu_back = jax.vjp(jax.nn.gelu, pre.astype(jnp.float32))
    grad_pre = gelu_back(grad_act)[0].astype(jnp.bfloat16).astype(jnp.float32)
    grad_second = jnp.einsum('tkgc,tgm->gkcm', grouped.astype(jnp.float32), grad_pre).reshape(BLOCKS, BW, HB)
    grad_mixed = jnp.einsum('tgm,gkcm->tkgc', grad_pre, second_view.astype(jnp.float32)).astype(jnp.bfloat16)
    grad_mixed = grad_mixed.reshape(count, BLOCKS, BW).astype(jnp.float32)
    blocked = inputs.reshape(count, BLOCKS, BW).astype(jnp.float32)
    grad_first = jnp.einsum('tki,tkj->kij', blocked, grad_mixed)
    back = jnp.einsum('tkj,kij->tki', grad_mixed, first.astype(jnp.float32)).reshape(count, D)
    grad_in = (upstream.astype(jnp.float32) + back).astype(jnp.bfloat16)
    grads = (grad_first, grad_second, grad_third, grad_fourth)
    return (grad_in, tuple((item.astype(jnp.bfloat16) for item in grads)))

def reference(tokens, cotangent, first_factor, second_factor, third_factor, fourth_factor):
    layer_inputs = []
    current = tokens
    outputs = []
    for layer in range(LAYERS):
        layer_inputs.append(current)
        current, unused = layer_forward(current, first_factor[layer], second_factor[layer], third_factor[layer], fourth_factor[layer])
        outputs.append(current)
    upstream = cotangent
    grads_in = [None] * LAYERS
    grads_w = [None] * LAYERS
    for layer in range(LAYERS - 1, -1, -1):
        weights = (first_factor[layer], second_factor[layer], third_factor[layer], fourth_factor[layer])
        unused, saved = layer_forward(layer_inputs[layer], *weights)
        upstream, grads = layer_backward(layer_inputs[layer], upstream, saved, *weights)
        grads_in[layer] = upstream
        grads_w[layer] = grads
    return (jnp.stack(outputs), jnp.stack(grads_in), jnp.stack([item[0] for item in grads_w]), jnp.stack([item[1] for item in grads_w]), jnp.stack([item[2] for item in grads_w]), jnp.stack([item[3] for item in grads_w]))
```

```python
import functools

import jax
import jax.numpy as jnp
from jax import lax
from jax.experimental import pallas as pl
from jax.experimental.pallas import tpu as pltpu
from jax.sharding import PartitionSpec as P

CHAINS = 1
VMEM_BYTES = 24 * 1024 * 1024
BF16 = jnp.bfloat16
F32 = jnp.float32
CUBIC = 0.044715
ROOT = 0.7978845608028654


def call(body, outs, *args):
    place = pl.BlockSpec(memory_space=pltpu.VMEM)
    scalar = pl.BlockSpec(memory_space=pltpu.SMEM)
    specs = [scalar if arg.dtype == jnp.int32 else place for arg in args]
    return pl.pallas_call(
        body,
        out_shape=[jax.ShapeDtypeStruct(shape, BF16) for shape in outs],
        in_specs=specs,
        out_specs=[place] * len(outs),
        compiler_params=pltpu.CompilerParams(vmem_limit_bytes=VMEM_BYTES),
    )(*args)


def dot(left, right):
    return lax.dot_general(left, right, (((1,), (0,)), ((), ())), preferred_element_type=F32)


def dot_nt(left, right):
    return lax.dot_general(left, right, (((1,), (1,)), ((), ())), preferred_element_type=F32)


def spots(rows, columns, row_key, column_key):
    row = lax.broadcasted_iota(jnp.int32, (rows, columns), 0)
    column = lax.broadcasted_iota(jnp.int32, (rows, columns), 1)
    return jnp.where(row_key(row) == column_key(column), 1.0, 0.0).astype(BF16)


def picks_first(k, inner):
    rows, columns = 512, 256

    def row_key(r):
        inside = r % (2 * inner)
        return jnp.where(inside // inner == k, (r // (2 * inner)) * inner + inside % inner, -1)

    return spots(rows, columns, row_key, lambda c: c)


def picks_second(g, inner):
    rows, columns = 512, 256
    half = 2 * inner

    def row_key(r):
        inside = r % (2 * half)
        return jnp.where(inside // half == g, (r // (2 * half)) * half + inside % half, -1)

    return spots(rows, columns, row_key, lambda c: c)


def prepare_first(w1, up, down):
    for k in range(2):
        pick = picks_first(k, 4)
        up[:, 256 * k : 256 * (k + 1)] = dot_nt(pick, w1[k]).astype(BF16)
        down[256 * k : 256 * (k + 1), :] = dot_nt(w1[k], pick).astype(BF16)


def prepare_second(w2, up, down):
    for g in range(2):
        pick = picks_second(g, 4)
        wide = dot(pick, w2[g]).astype(BF16)
        down[:, 1024 * g : 1024 * (g + 1)] = wide
        up[1024 * g : 1024 * (g + 1), :] = wide.T


def enter(x, w1_up, mixed):
    mixed[...] = dot(w1_up[...], x[...]).astype(BF16).reshape(mixed.shape)


def enter_choice(choose, arrived, x, w1_up, x_now, mixed):
    now = jnp.where(choose[0] > 0, arrived[...], x[...])
    x_now[...] = now
    mixed[...] = dot(w1_up[...], now).astype(BF16).reshape(mixed.shape)


def gelu_tanh(value):
    return jnp.tanh(ROOT * (value + CUBIC * (value * value * value)))


def middle(arrived, w2_up, w3_up, spread, *kept):
    joined = arrived[...].reshape(512, arrived.shape[2])
    for g in range(2):
        pre = dot(w2_up[1024 * g : 1024 * (g + 1), :], joined).astype(BF16)
        wide = pre.astype(F32)
        activated = (0.5 * wide * (1.0 + gelu_tanh(wide))).astype(BF16)
        if kept:
            kept[0][g] = pre
            kept[1][g] = activated
        out = dot(w3_up[g], activated).astype(BF16)
        spread[:, 32 * g : 32 * (g + 1), :] = out.reshape(32, 32, out.shape[1])


def leave(arrived, w4_up, x, out):
    for k in range(2):
        rows = slice(256 * k, 256 * (k + 1))
        part = arrived[...].reshape(64, 32, arrived.shape[2])[:, 16 * k : 16 * (k + 1), :]
        total = dot(w4_up[k], part.reshape(1024, part.shape[2]))
        out[rows, :] = (x[rows, :].astype(F32) + total).astype(BF16)


def back_enter_from(now, w4, spread):
    parts = []
    for k in range(2):
        part = dot(w4[k], now[256 * k : 256 * (k + 1), :]).astype(BF16)
        parts.append(part.reshape(64, 1, 16, part.shape[1]))
    joined = jnp.concatenate(parts, axis=1)
    spread[...] = joined.reshape(spread.shape)


def back_enter(upstream, w4, spread):
    back_enter_from(upstream[...], w4, spread)


def back_enter_choice(choose, arrived, upstream, w4, now_out, spread):
    now = jnp.where(choose[0] > 0, arrived[...], upstream[...])
    now_out[...] = now
    back_enter_from(now, w4, spread)


def back_middle(arrived, w3, w2_down, pre, back, *kept):
    total = None
    for g in range(2):
        part = arrived[:, 32 * g : 32 * (g + 1), :]
        part = part.reshape(1024, part.shape[2])
        grad = dot(w3[g], part)
        value = pre[g].astype(F32)
        bend = gelu_tanh(value)
        slope = ROOT * (1.0 + 3.0 * CUBIC * (value * value))
        factor = 0.5 * (1.0 + bend) + (0.5 * value * (1.0 - bend * bend)) * slope
        grad_pre = (grad * factor).astype(BF16)
        if kept:
            kept[0][g] = grad_pre
        term = dot(w2_down[:, 1024 * g : 1024 * (g + 1)], grad_pre)
        total = term if total is None else total + term
    back[...] = total.astype(BF16).reshape(back.shape)


def back_leave(arrived, w1_down, upstream, out):
    total = dot(w1_down[...], arrived[...].reshape(512, arrived.shape[2]))
    out[...] = (upstream[...].astype(F32) + total).astype(BF16)


def grads_fourth(arrived, up, grad):
    for k in range(2):
        part = arrived[...].reshape(64, 32, arrived.shape[2])[:, 16 * k : 16 * (k + 1), :]
        part = part.reshape(1024, part.shape[2])
        grad[k] = dot_nt(part, up[256 * k : 256 * (k + 1), :]).astype(BF16)


def grads_third(act, back, grad):
    for g in range(2):
        part = back[:, 32 * g : 32 * (g + 1), :]
        part = part.reshape(1024, part.shape[2])
        for start in range(0, 1024, 256):
            grad[g, start : start + 256, :] = dot_nt(act[g, start : start + 256, :], part).astype(BF16)


def grads_second(mixed, pre, grad):
    for g in range(2):
        total = dot_nt(mixed[...].reshape(512, mixed.shape[2]), pre[g])
        total = total.reshape(32, 16, 1024)[:, 8 * g : 8 * (g + 1), :]
        grad[g] = total.reshape(256, 1024).astype(BF16)


def grads_first(x, back, grad):
    for k in range(2):
        pick = picks_first(k, 4)
        term = dot_nt(x[256 * k : 256 * (k + 1), :], back[...].reshape(512, back.shape[2]))
        grad[k] = dot(term.astype(BF16), pick).astype(BF16)


def exchange(block):
    return lax.all_to_all(block, "blk", split_axis=0, concat_axis=0, tiled=True)


def shards(tokens, cotangent, first_factor, second_factor, third_factor, fourth_factor):
    segments = lax.axis_size("segment")
    position = lax.axis_index("segment")
    total = tokens.shape[0]
    part = total // CHAINS
    w1, w2, w3, w4 = first_factor[0], second_factor[0], third_factor[0], fourth_factor[0]
    w1_up, w1_down = call(prepare_first, [(512, 512), (512, 512)], w1)
    entry = tokens.T
    x = [entry[:, part * h : part * (h + 1)] for h in range(CHAINS)]
    w2_up, w2_down = call(prepare_second, [(2048, 512), (512, 2048)], w2)
    w3_up = w3.transpose(0, 2, 1)
    w4_up = w4.transpose(0, 2, 1)

    chunk = (32, 16, part)
    wide = (32, 64, part)
    flat = (512, part)
    inner = (2, 1024, part)
    mixed_in = [None] * CHAINS
    pres = [None] * CHAINS
    acts = [None] * CHAINS
    spreads = [None] * CHAINS
    outs = [None] * CHAINS
    incoming = [None] * CHAINS
    for step in range(segments):
        last = step == segments - 1
        choose = (position == step).astype(jnp.int32).reshape(1)
        for h in range(CHAINS):
            if step == 0:
                (mixed,) = call(enter, [chunk], x[h], w1_up)
            else:
                x[h], mixed = call(enter_choice, [flat, chunk], choose, incoming[h], x[h], w1_up)
            arrived = exchange(mixed)
            if last:
                mixed_in[h] = arrived
                spread, pres[h], acts[h] = call(middle, [wide, inner, inner], arrived, w2_up, w3_up)
            else:
                (spread,) = call(middle, [wide], arrived, w2_up, w3_up)
            arrived = exchange(spread)
            (outs[h],) = call(leave, [flat], arrived, w4_up, x[h])
            if last:
                spreads[h] = arrived
            else:
                incoming[h] = lax.ppermute(outs[h], "segment", [(step, step + 1)])

    returning = cotangent.T
    up = [returning[:, part * h : part * (h + 1)] for h in range(CHAINS)]
    back_spread = [None] * CHAINS
    grad_pres = [None] * CHAINS
    back_mixed = [None] * CHAINS
    grads = [None] * CHAINS
    for step in range(segments):
        last = step == segments - 1
        choose = (position == segments - 1 - step).astype(jnp.int32).reshape(1)
        for h in range(CHAINS):
            if step == 0:
                (spread,) = call(back_enter, [wide], up[h], w4)
            else:
                up[h], spread = call(back_enter_choice, [flat, wide], choose, incoming[h], up[h], w4)
            back_spread[h] = exchange(spread)
            if last:
                back, grad_pres[h] = call(
                    back_middle, [chunk, inner], back_spread[h], w3, w2_down, pres[h]
                )
            else:
                (back,) = call(back_middle, [chunk], back_spread[h], w3, w2_down, pres[h])
            back_mixed[h] = exchange(back)
            (grads[h],) = call(back_leave, [flat], back_mixed[h], w1_down, up[h])
            if not last:
                source = segments - 1 - step
                incoming[h] = lax.ppermute(grads[h], "segment", [(source, source - 1)])

    (fourth_grad,) = call(grads_fourth, [w4.shape], *spreads, *up)
    (third_grad,) = call(grads_third, [w3.shape], *acts, *back_spread)
    (second_grad,) = call(grads_second, [w2.shape], *mixed_in, *grad_pres)
    (first_grad,) = call(grads_first, [w1.shape], *x, *back_mixed)
    segment_outputs = jnp.concatenate([out.T for out in outs], axis=0)
    input_grads = jnp.concatenate([grad.T for grad in grads], axis=0)
    return (
        segment_outputs[None],
        input_grads[None],
        first_grad[None],
        second_grad[None],
        third_grad[None],
        fourth_grad[None],
    )


def solution(mesh):
    placed = (
        P(None, "blk"),
        P(None, "blk"),
        P("segment", "blk", None, None),
        P("segment", "blk", None, None),
        P("segment", "blk", None, None),
        P("segment", "blk", None, None),
    )
    return jax.shard_map(
        shards,
        mesh=mesh,
        in_specs=placed,
        out_specs=(
            P("segment", None, "blk"),
            P("segment", None, "blk"),
            P("segment", "blk", None, None),
            P("segment", "blk", None, None),
            P("segment", "blk", None, None),
            P("segment", "blk", None, None),
        ),
        check_vma=False,
    )
```

```python
import functools

import jax
import jax.numpy as jnp
from jax import lax
from jax.experimental import pallas as pl
from jax.experimental.pallas import tpu as pltpu
from jax.sharding import PartitionSpec as P

VMEM_BYTES = 12 * 1024 * 1024
BF16 = jnp.bfloat16
F32 = jnp.float32
CUBIC = 0.044715
ROOT = 0.7978845608028654
COUNT = 256
PEERS = 32
FLAT = (512, COUNT)
CHUNK = (PEERS, 16, COUNT)
WIDE = (PEERS, 64, COUNT)
INNER = (2, 1024, COUNT)
PARTS = (2, 256, COUNT)


class Near:
    def __init__(self, value):
        self.value = value


class Far:
    def __init__(self, value):
        self.value = value


def call(body, outs, *args, scratch=()):
    place = pl.BlockSpec(memory_space=pltpu.VMEM)
    scalar = pl.BlockSpec(memory_space=pltpu.SMEM)
    specs, operands = [], []
    for arg in args:
        if isinstance(arg, Near):
            specs.append(place)
            operands.append(pltpu.with_memory_space_constraint(arg.value, pltpu.VMEM))
        elif isinstance(arg, Far):
            specs.append(pl.BlockSpec(memory_space=pltpu.HBM))
            operands.append(pltpu.with_memory_space_constraint(arg.value, pltpu.HBM))
        else:
            specs.append(scalar if arg.dtype == jnp.int32 else place)
            operands.append(arg)
    shapes = [
        pltpu.VMEM(out.value, BF16) if isinstance(out, Near) else jax.ShapeDtypeStruct(out, BF16)
        for out in outs
    ]
    return pl.pallas_call(
        body,
        out_shape=shapes,
        in_specs=specs,
        out_specs=[place] * len(outs),
        scratch_shapes=list(scratch),
        compiler_params=pltpu.CompilerParams(vmem_limit_bytes=VMEM_BYTES),
    )(*operands)


def load_body(*refs):
    sources, plain, turned_refs, done = refs[0:4], refs[4:8], refs[8:12], refs[12]
    copies = [
        pltpu.make_async_copy(source, target, done.at[i])
        for i, (source, target) in enumerate(zip(sources, plain))
    ]
    for copy in copies:
        copy.start()
    for copy, source, target in zip(copies, plain, turned_refs):
        copy.wait()
        for b in range(2):
            target[b] = source[b].T


def load(*weights):
    shapes = [w.shape for w in weights]
    shapes += [(w.shape[0], w.shape[2], w.shape[1]) for w in weights]
    return pl.pallas_call(
        load_body,
        out_shape=[pltpu.VMEM(shape, BF16) for shape in shapes],
        in_specs=[pl.BlockSpec(memory_space=pltpu.HBM)] * 4,
        out_specs=[pl.BlockSpec(memory_space=pltpu.VMEM)] * 8,
        scratch_shapes=[pltpu.SemaphoreType.DMA((4,))],
        compiler_params=pltpu.CompilerParams(vmem_limit_bytes=VMEM_BYTES),
    )(*[pltpu.with_memory_space_constraint(w, pltpu.HBM) for w in weights])


def dot(left, right):
    return lax.dot_general(left, right, (((1,), (0,)), ((), ())), preferred_element_type=F32)


def dot_nt(left, right):
    return lax.dot_general(left, right, (((1,), (1,)), ((), ())), preferred_element_type=F32)


def upper_rows(shape):
    return lax.rem(lax.broadcasted_iota(jnp.int32, shape, 0), 8) < 4


def interleave(a, b):
    upper = upper_rows(a.shape)
    first = jnp.where(upper, a, pltpu.roll(b, 4, 0))
    second = jnp.where(upper, pltpu.roll(a, 252, 0), b)
    return stack_halves(first, second)


def stack_halves(first, second):
    tiles = [item.reshape(PEERS, 1, 8, COUNT) for item in (first, second)]
    return jnp.concatenate(tiles, axis=1).reshape(CHUNK).astype(BF16)


def halves_of(joined):
    tiles = joined.astype(F32).reshape(PEERS, 2, 8, COUNT)
    return [tiles[:, g].reshape(256, COUNT) for g in range(2)]


def separate(joined):
    first, second = halves_of(joined)
    upper = upper_rows(first.shape)
    a = jnp.where(upper, first, pltpu.roll(second, 4, 0))
    b = jnp.where(upper, pltpu.roll(first, 252, 0), second)
    return a.astype(BF16), b.astype(BF16)


def enter(tokens, w1_up, x, mixed):
    x[...] = tokens[...].T
    mixed[...] = interleave(*[dot(w1_up[k], x[256 * k : 256 * (k + 1), :]) for k in range(2)])


def gelu_tanh(value):
    return jnp.tanh(ROOT * (value + CUBIC * (value * value * value)))


def gelu(value):
    return 0.5 * value * (1.0 + gelu_tanh(value))


def gelu_slope(value):
    bend = gelu_tanh(value)
    slope = ROOT * (1.0 + 3.0 * CUBIC * (value * value))
    return 0.5 * (1.0 + bend) + (0.5 * value * (1.0 - bend * bend)) * slope


def middle(arrived, w2_up, w3_up, spread, *kept):
    joined = [half.astype(BF16) for half in halves_of(arrived[...])]
    for g in range(2):
        pre = dot(w2_up[g], joined[g]).astype(BF16)
        act = gelu(pre.astype(F32)).astype(BF16)
        if kept:
            kept[0][g] = pre
            kept[1][g] = act
        out = dot(w3_up[g], act).astype(BF16)
        spread[:, 32 * g : 32 * (g + 1), :] = out.reshape(PEERS, 32, COUNT)


def middle_or_first(plane, here, arrived, w2_up, w3_up, far_tokens, w4, spread, up, tokens, done):
    @pl.when(here[0] == plane)
    def _():
        copy = pltpu.make_async_copy(far_tokens, tokens, done)
        copy.start()
        copy.wait()
        up[...] = tokens[...].T
        back_spread(up, w4, spread)

    @pl.when(here[0] != plane)
    def _():
        up[...] = jnp.zeros_like(up)
        middle(arrived, w2_up, w3_up, spread)


def leave_rows(arrived, w4_up, x, out):
    rows = arrived[...].reshape(64, 32, COUNT)
    for k in range(2):
        part = rows[:, 16 * k : 16 * (k + 1), :].reshape(1024, COUNT)
        place = slice(256 * k, 256 * (k + 1))
        out[place, :] = (x[place, :].astype(F32) + dot(w4_up[k], part)).astype(BF16)


def leave(arrived, x, w4_up, out):
    leave_rows(arrived, w4_up, x, out)


def enter_choice(plane, here, incoming, held, w1_up, x, mixed):
    x[...] = jnp.where(here[0] == plane, incoming[...], held[...])
    mixed[...] = interleave(*[dot(w1_up[k], x[256 * k : 256 * (k + 1), :]) for k in range(2)])


def back_spread(up, w4, spread):
    parts = []
    for k in range(2):
        part = dot(w4[k], up[256 * k : 256 * (k + 1), :]).astype(BF16)
        parts.append(part.reshape(64, 1, 16, COUNT))
    spread[...] = jnp.concatenate(parts, axis=1).reshape(WIDE)


def unmix(joined, w1, up, out):
    for k, part in enumerate(separate(joined)):
        rows = slice(256 * k, 256 * (k + 1))
        out[rows, :] = (up[rows, :].astype(F32) + dot(w1[k], part)).astype(BF16)


def back_enter_choice(plane, here, incoming, held, w4, up, spread):
    up[...] = jnp.where(here[0] == plane, incoming[...], held[...])
    back_spread(up, w4, spread)


def back_enter_or_last(plane, here, ready, incoming, held, w4, up, spread):
    @pl.when(here[0] == plane + 1)
    def _():
        up[...] = held[...]
        spread[...] = ready[...]

    @pl.when(here[0] != plane + 1)
    def _():
        back_enter_choice(plane, here, incoming, held, w4, up, spread)


def back_step(arrived, up, w1, out):
    unmix(arrived[...], w1, up, out)


def back_leave(arrived, up, w1, out, parts):
    for k, part in enumerate(separate(arrived[...])):
        parts[k] = part
        rows = slice(256 * k, 256 * (k + 1))
        total = up[rows, :].astype(F32) + dot(w1[k], part)
        out[:, rows] = total.astype(BF16).T


def back_middle(arrived, pre, w2, w3, back, *kept):
    terms = []
    for g in range(2):
        part = arrived[:, 32 * g : 32 * (g + 1), :].reshape(1024, COUNT)
        grad_pre = (dot(w3[g], part) * gelu_slope(pre[g].astype(F32))).astype(BF16)
        if kept:
            kept[0][g] = grad_pre
        terms.append(dot(w2[g], grad_pre))
    back[...] = stack_halves(*terms)


def leave_and_fourth(plane, here, rows_new, rows_held, x, w4_up, up, out, grad):
    rows = jnp.where(here[0] == plane, rows_new[...], rows_held[...])
    rows = rows.reshape(64, 32, COUNT)
    for k in range(2):
        part = rows[:, 16 * k : 16 * (k + 1), :].reshape(1024, COUNT)
        place = slice(256 * k, 256 * (k + 1))
        total = x[place, :].astype(F32) + dot(w4_up[k], part)
        out[:, place] = total.astype(BF16).T
        grad[k] = dot_nt(part, up[place, :]).astype(BF16)


def grads_third(act, back, grad):
    for g in range(2):
        part = back[:, 32 * g : 32 * (g + 1), :].reshape(1024, COUNT)
        for start in range(0, 1024, 256):
            rows = slice(start, start + 256)
            grad[g, rows, :] = dot_nt(act[g, rows, :], part).astype(BF16)


def grads_second(mixed, pre, grad):
    for g, part in enumerate(halves_of(mixed[...])):
        grad[g] = dot_nt(part.astype(BF16), pre[g]).astype(BF16)


def grads_first(x, back, grad):
    for k in range(2):
        grad[k] = dot_nt(x[256 * k : 256 * (k + 1), :], back[k]).astype(BF16)


def exchange(block):
    return lax.all_to_all(block, "blk", split_axis=0, concat_axis=0, tiled=True)


def shards(tokens, cotangent, first_factor, second_factor, third_factor, fourth_factor):
    segments = lax.axis_size("segment")
    position = lax.axis_index("segment")
    own = (first_factor[0], second_factor[0], third_factor[0], fourth_factor[0])

    here = position.astype(jnp.int32).reshape(1)
    tokens, here = lax.optimization_barrier((tokens, here))
    w1, w2, w3, w4, w1_up, w2_up, w3_up, w4_up = [Near(item) for item in load(*own)]

    for step in range(segments):
        if step == 0:
            x, mixed = call(enter, [Near(FLAT), Near(CHUNK)], tokens, w1_up)
        else:
            x, mixed = call(
                functools.partial(enter_choice, step),
                [Near(FLAT), Near(CHUNK)],
                here,
                Near(incoming),
                Near(x),
                w1_up,
            )
        arrived = exchange(mixed)
        if step < segments - 2:
            (spread,) = call(middle, [Near(WIDE)], Near(arrived), w2_up, w3_up)
        elif step == segments - 2:
            spread, up = call(
                functools.partial(middle_or_first, segments - 1),
                [Near(WIDE), Near(FLAT)],
                here,
                Near(arrived),
                w2_up,
                w3_up,
                Far(cotangent),
                w4,
                scratch=[pltpu.VMEM((COUNT, 512), BF16), pltpu.SemaphoreType.DMA],
            )
        else:
            spread, pre, act = call(
                middle,
                [Near(WIDE), Near(INNER), Near(INNER)],
                Near(arrived),
                w2_up,
                w3_up,
            )
            break
        rows = exchange(spread)
        (out,) = call(leave, [Near(FLAT)], Near(rows), Near(x), w4_up)
        incoming = lax.ppermute(out, "segment", [(step, step + 1)])

    mixed_in, gathered = arrived, rows
    for step in range(segments):
        last = step == segments - 1
        plane = segments - 1 - step
        if step == 1:
            up, spread = call(
                functools.partial(back_enter_or_last, plane),
                [Near(FLAT), Near(WIDE)],
                here,
                Near(spread),
                Near(incoming),
                Near(up),
                w4,
            )
            rows_last = gathered = exchange(spread)
        elif step:
            up, spread = call(
                functools.partial(back_enter_choice, plane),
                [Near(FLAT), Near(WIDE)],
                here,
                Near(incoming),
                Near(up),
                w4,
            )
            gathered = exchange(spread)
        shapes = [CHUNK, INNER] if last else [Near(CHUNK)]
        results = call(back_middle, shapes, Near(gathered), Near(pre), w2, w3)
        arrived = exchange(results[0])
        if not last:
            (grad_in,) = call(back_step, [Near(FLAT)], Near(arrived), Near(up), w1)
            incoming = lax.ppermute(grad_in, "segment", [(plane, plane - 1)])

    grad_pre = results[1]
    segment_outputs, fourth_grad = call(
        functools.partial(leave_and_fourth, segments - 1),
        [(COUNT, 512), own[3].shape],
        here,
        rows_last,
        rows,
        x,
        w4_up,
        up,
    )
    (third_grad,) = call(grads_third, [own[2].shape], act, gathered)
    (second_grad,) = call(grads_second, [own[1].shape], mixed_in, grad_pre)
    grad_in, parts = call(back_leave, [(COUNT, 512), PARTS], arrived, up, own[0])
    (first_grad,) = call(grads_first, [own[0].shape], x, parts)
    return (
        segment_outputs[None],
        grad_in[None],
        first_grad[None],
        second_grad[None],
        third_grad[None],
        fourth_grad[None],
    )


def solution(mesh):
    placed = (
        P(None, "blk"),
        P(None, "blk"),
        P("segment", "blk", None, None),
        P("segment", "blk", None, None),
        P("segment", "blk", None, None),
        P("segment", "blk", None, None),
    )
    return jax.shard_map(
        shards,
        mesh=mesh,
        in_specs=placed,
        out_specs=(
            P("segment", None, "blk"),
            P("segment", None, "blk"),
            P("segment", "blk", None, None),
            P("segment", "blk", None, None),
            P("segment", "blk", None, None),
            P("segment", "blk", None, None),
        ),
        check_vma=False,
    )
```

```python
import functools

import jax
import jax.numpy as jnp
from jax import lax
from jax.experimental import pallas as pl
from jax.experimental.pallas import tpu as pltpu
from jax.sharding import PartitionSpec as P

VMEM_BYTES = 12 * 1024 * 1024
BF16 = jnp.bfloat16
F32 = jnp.float32
CUBIC = 0.044715
ROOT = 0.7978845608028654
COUNT = 256
PEERS = 32
FLAT = (512, COUNT)
CHUNK = (PEERS, 16, COUNT)
WIDE = (PEERS, 64, COUNT)
INNER = (2, 1024, COUNT)
PARTS = (2, 256, COUNT)


class Near:
    def __init__(self, value, kind=BF16):
        self.value = value
        self.kind = kind


class Far:
    def __init__(self, value):
        self.value = value


def call(body, outs, *args, scratch=(), copies=0, limit=VMEM_BYTES):
    place = pl.BlockSpec(memory_space=pltpu.VMEM)
    scalar = pl.BlockSpec(memory_space=pltpu.SMEM)
    far = pl.BlockSpec(memory_space=pltpu.HBM)
    specs, operands = [], []
    for arg in args:
        if isinstance(arg, Near):
            specs.append(place)
            operands.append(pltpu.with_memory_space_constraint(arg.value, pltpu.VMEM))
        elif isinstance(arg, Far):
            specs.append(far)
            operands.append(pltpu.with_memory_space_constraint(arg.value, pltpu.HBM))
        else:
            specs.append(scalar if arg.dtype == jnp.int32 else place)
            operands.append(arg)
    shapes, places = [], []
    for out in outs:
        if isinstance(out, Near):
            shapes.append(pltpu.VMEM(out.value, out.kind))
        elif isinstance(out, Far):
            shapes.append(pltpu.HBM(out.value, BF16))
        else:
            shapes.append(jax.ShapeDtypeStruct(out, BF16))
        places.append(far if isinstance(out, Far) else place)
    scratch_shapes = [pltpu.VMEM(shape, BF16) for shape in scratch]
    if copies:
        scratch_shapes.append(pltpu.SemaphoreType.DMA((copies,)))
    return pl.pallas_call(
        body,
        out_shape=shapes,
        in_specs=specs,
        out_specs=places,
        scratch_shapes=scratch_shapes,
        compiler_params=pltpu.CompilerParams(vmem_limit_bytes=limit),
    )(*operands)


class Copies:
    def __init__(self, done):
        self.done = done
        self.count = 0

    def start(self, source, target):
        copy = pltpu.make_async_copy(source, target, self.done.at[self.count])
        self.count += 1
        copy.start()
        return copy


def load_enter(tokens_far, *refs):
    sources, plain, turned = refs[0:4], refs[4:8], refs[8:12]
    x, mixed, tokens, done = refs[12:]
    copies = Copies(done)
    came = copies.start(tokens_far, tokens)
    ready = {}
    for i in (0, 2, 1, 3):
        ready[i] = [copies.start(sources[i].at[b], plain[i].at[b]) for b in range(2)]
    came.wait()
    x[...] = tokens[...].T
    for i in (0, 2, 1, 3):
        for b in range(2):
            ready[i][b].wait()
            turned[i][b] = plain[i][b].T
        if i == 0:
            mixed[...] = interleave(
                *[dot(turned[0][k], x[256 * k : 256 * (k + 1), :]) for k in range(2)]
            )


def dot(left, right):
    return lax.dot_general(left, right, (((1,), (0,)), ((), ())), preferred_element_type=F32)


def dot_nt(left, right):
    return lax.dot_general(left, right, (((1,), (1,)), ((), ())), preferred_element_type=F32)


def upper_rows(shape):
    return lax.rem(lax.broadcasted_iota(jnp.int32, shape, 0), 8) < 4


def interleave(a, b):
    upper = upper_rows(a.shape)
    first = jnp.where(upper, a, pltpu.roll(b, 4, 0))
    second = jnp.where(upper, pltpu.roll(a, 252, 0), b)
    return stack_halves(first, second)


def stack_halves(first, second):
    tiles = [item.reshape(PEERS, 1, 8, COUNT) for item in (first, second)]
    return jnp.concatenate(tiles, axis=1).reshape(CHUNK).astype(BF16)


def halves_of(joined):
    tiles = joined.astype(F32).reshape(PEERS, 2, 8, COUNT)
    return [tiles[:, g].reshape(256, COUNT) for g in range(2)]


def separate(joined):
    first, second = halves_of(joined)
    upper = upper_rows(first.shape)
    a = jnp.where(upper, first, pltpu.roll(second, 4, 0))
    b = jnp.where(upper, pltpu.roll(first, 252, 0), second)
    return a.astype(BF16), b.astype(BF16)


def gelu_tanh(value):
    return jnp.tanh(ROOT * (value + CUBIC * (value * value * value)))


def gelu(value):
    return 0.5 * value * (1.0 + gelu_tanh(value))


def gelu_slope(value, bend):
    slope = ROOT * (1.0 + 3.0 * CUBIC * (value * value))
    return 0.5 * (1.0 + bend) + (0.5 * value * (1.0 - bend * bend)) * slope


def middle(arrived, w2_up, w3_up, spread):
    joined = [half.astype(BF16) for half in halves_of(arrived[...])]
    for g in range(2):
        pre = dot(w2_up[g], joined[g]).astype(BF16)
        act = gelu(pre.astype(F32)).astype(BF16)
        out = dot(w3_up[g], act).astype(BF16)
        spread[:, 32 * g : 32 * (g + 1), :] = out.reshape(PEERS, 32, COUNT)


def middle_kept(arrived, w2_up, w3_up, spread, slope, mixed_far, act_far, act, done):
    copies = Copies(done)
    leaving = [copies.start(arrived, mixed_far)]
    joined = [half.astype(BF16) for half in halves_of(arrived[...])]
    for g in range(2):
        pre = dot(w2_up[g], joined[g]).astype(BF16).astype(F32)
        bend = gelu_tanh(pre)
        act[g] = (0.5 * pre * (1.0 + bend)).astype(BF16)
        leaving.append(copies.start(act.at[g], act_far.at[g]))
        slope[g] = gelu_slope(pre, bend)
        out = dot(w3_up[g], act[g]).astype(BF16)
        spread[:, 32 * g : 32 * (g + 1), :] = out.reshape(PEERS, 32, COUNT)
    for copy in leaving:
        copy.wait()


def middle_or_first(plane, here, arrived, w2_up, w3_up, far_tokens, w4, spread, up, tokens, done):
    @pl.when(here[0] == plane)
    def _():
        Copies(done).start(far_tokens, tokens).wait()
        up[...] = tokens[...].T
        back_spread(up, w4, spread)

    @pl.when(here[0] != plane)
    def _():
        up[...] = jnp.zeros_like(up)
        middle(arrived, w2_up, w3_up, spread)


def leave_rows(arrived, w4_up, x, out):
    rows = arrived[...].reshape(64, 32, COUNT)
    for k in range(2):
        part = rows[:, 16 * k : 16 * (k + 1), :].reshape(1024, COUNT)
        place = slice(256 * k, 256 * (k + 1))
        out[place, :] = (x[place, :].astype(F32) + dot(w4_up[k], part)).astype(BF16)


def leave(arrived, x, w4_up, out):
    leave_rows(arrived, w4_up, x, out)


def enter_choice(plane, here, incoming, held, w1_up, x, mixed):
    x[...] = jnp.where(here[0] == plane, incoming[...], held[...])
    mixed[...] = interleave(*[dot(w1_up[k], x[256 * k : 256 * (k + 1), :]) for k in range(2)])


def back_spread(up, w4, spread):
    parts = []
    for k in range(2):
        part = dot(w4[k], up[256 * k : 256 * (k + 1), :]).astype(BF16)
        parts.append(part.reshape(64, 1, 16, COUNT))
    spread[...] = jnp.concatenate(parts, axis=1).reshape(WIDE)


def unmix(joined, w1, up, out):
    for k, part in enumerate(separate(joined)):
        rows = slice(256 * k, 256 * (k + 1))
        out[rows, :] = (up[rows, :].astype(F32) + dot(w1[k], part)).astype(BF16)


def back_enter_choice(plane, here, incoming, held, w4, up, spread):
    up[...] = jnp.where(here[0] == plane, incoming[...], held[...])
    back_spread(up, w4, spread)


def back_enter_or_last(plane, here, ready, incoming, held, w4, up, spread):
    @pl.when(here[0] == plane + 1)
    def _():
        up[...] = held[...]
        spread[...] = ready[...]

    @pl.when(here[0] != plane + 1)
    def _():
        back_enter_choice(plane, here, incoming, held, w4, up, spread)


def back_step(arrived, up, w1, out):
    unmix(arrived[...], w1, up, out)


def back_product(arrived, slope, w2, w3, g):
    part = arrived[:, 32 * g : 32 * (g + 1), :].reshape(1024, COUNT)
    grad_pre = (dot(w3[g], part) * slope[g]).astype(BF16)
    return grad_pre, dot(w2[g], grad_pre)


def back_middle(arrived, slope, w2, w3, back):
    back[...] = stack_halves(*[back_product(arrived, slope, w2, w3, g)[1] for g in range(2)])


def back_middle_kept(arrived, slope, w2, w3, back, arrived_far, pre_far, grad_pre, done):
    copies = Copies(done)
    leaving = [copies.start(arrived, arrived_far)]
    terms = []
    for g in range(2):
        grad_pre[g], term = back_product(arrived, slope, w2, w3, g)
        leaving.append(copies.start(grad_pre.at[g], pre_far.at[g]))
        terms.append(term)
    back[...] = stack_halves(*terms)
    for copy in leaving:
        copy.wait()


def gradients(plane, here, *refs):
    new_in, held_in, x_in, w4_in, up_in, act_in, back_in, mixed_in, pre_in = refs[0:9]
    out_far, fourth_far, third_far, second_far = refs[9:13]
    rows, x, w4, up, act, back, mixed, pre, out, fourth, third, second, done = refs[13:]
    copies = Copies(done)
    act_ready = copies.start(act_in, act)
    back_ready = copies.start(back_in, back)
    ready = [copies.start(mixed_in, mixed), copies.start(pre_in, pre)]
    ready += [copies.start(x_in, x), copies.start(up_in, up), copies.start(w4_in, w4)]
    rows_done = done.at[copies.count]
    copies.count += 1

    @pl.when(here[0] == plane)
    def _():
        pltpu.make_async_copy(new_in, rows, rows_done).start()

    @pl.when(here[0] != plane)
    def _():
        pltpu.make_async_copy(held_in, rows, rows_done).start()

    leaving = []
    act_ready.wait()
    back_ready.wait()
    for g in range(2):
        part = back[:, 32 * g : 32 * (g + 1), :].reshape(1024, COUNT)
        for half in range(2):
            band = pl.ds(512 * half, 512)
            for start in (512 * half, 512 * half + 256):
                place = slice(start, start + 256)
                third[g, place, :] = dot_nt(act[g, place, :], part).astype(BF16)
            leaving.append(copies.start(third.at[g, band], third_far.at[g, band]))
    for copy in ready:
        copy.wait()
    for g, part in enumerate(halves_of(mixed[...])):
        second[g] = dot_nt(part.astype(BF16), pre[g]).astype(BF16)
        leaving.append(copies.start(second.at[g], second_far.at[g]))
    pltpu.make_async_copy(held_in, rows, rows_done).wait()
    joined = rows[...].reshape(64, 32, COUNT)
    for k in range(2):
        part = joined[:, 16 * k : 16 * (k + 1), :].reshape(1024, COUNT)
        place = slice(256 * k, 256 * (k + 1))
        fourth[k] = dot_nt(part, up[place, :]).astype(BF16)
        leaving.append(copies.start(fourth.at[k], fourth_far.at[k]))
        total = x[place, :].astype(F32) + dot(w4[k].T, part)
        out[:, place] = total.astype(BF16).T
    leaving.append(copies.start(out, out_far))
    for copy in leaving:
        copy.wait()


def back_leave(arrived, up, w1, x, out, grad):
    for k, part in enumerate(separate(arrived[...])):
        place = slice(256 * k, 256 * (k + 1))
        total = up[place, :].astype(F32) + dot(w1[k], part)
        out[:, place] = total.astype(BF16).T
        grad[k] = dot_nt(x[place, :], part).astype(BF16)


def exchange(block):
    return lax.all_to_all(block, "blk", split_axis=0, concat_axis=0, tiled=True)


def shards(tokens, cotangent, first_factor, second_factor, third_factor, fourth_factor):
    segments = lax.axis_size("segment")
    position = lax.axis_index("segment")
    own = (first_factor[0], second_factor[0], third_factor[0], fourth_factor[0])

    here = position.astype(jnp.int32).reshape(1)
    tokens, here = lax.optimization_barrier((tokens, here))
    flipped = [(w.shape[0], w.shape[2], w.shape[1]) for w in own]
    results = call(
        load_enter,
        [Near(w.shape) for w in own] + [Near(f) for f in flipped] + [Near(FLAT), Near(CHUNK)],
        Far(tokens),
        *[Far(w) for w in own],
        scratch=[(COUNT, 512)],
        copies=9,
    )
    w1, w2, w3, w4, w1_up, w2_up, w3_up, w4_up = [Near(item) for item in results[:8]]
    x, mixed = results[8:]

    for step in range(segments):
        if step:
            x, mixed = call(
                functools.partial(enter_choice, step),
                [Near(FLAT), Near(CHUNK)],
                here,
                Near(incoming),
                Near(x),
                w1_up,
            )
        arrived = exchange(mixed)
        if step < segments - 2:
            (spread,) = call(middle, [Near(WIDE)], Near(arrived), w2_up, w3_up)
        elif step == segments - 2:
            spread, up = call(
                functools.partial(middle_or_first, segments - 1),
                [Near(WIDE), Near(FLAT)],
                here,
                Near(arrived),
                w2_up,
                w3_up,
                Far(cotangent),
                w4,
                scratch=[(COUNT, 512)],
                copies=1,
            )
        else:
            spread, slope, mixed_in, act = call(
                middle_kept,
                [Near(WIDE), Near(INNER, F32), Far(CHUNK), Far(INNER)],
                Near(arrived),
                w2_up,
                w3_up,
                scratch=[INNER],
                copies=3,
            )
            break
        rows = exchange(spread)
        (out,) = call(leave, [Near(FLAT)], Near(rows), Near(x), w4_up)
        incoming = lax.ppermute(out, "segment", [(step, step + 1)])

    gathered = rows
    for step in range(segments):
        last = step == segments - 1
        plane = segments - 1 - step
        if step == 1:
            up, spread = call(
                functools.partial(back_enter_or_last, plane),
                [Near(FLAT), Near(WIDE)],
                here,
                Near(spread),
                Near(incoming),
                Near(up),
                w4,
            )
            rows_last = gathered = exchange(spread)
        elif step:
            up, spread = call(
                functools.partial(back_enter_choice, plane),
                [Near(FLAT), Near(WIDE)],
                here,
                Near(incoming),
                Near(up),
                w4,
            )
            gathered = exchange(spread)
        factors = (Near(gathered), Near(slope), w2, w3)
        if last:
            break
        (back,) = call(back_middle, [Near(CHUNK)], *factors)
        arrived = exchange(back)
        (grad_in,) = call(back_step, [Near(FLAT)], Near(arrived), Near(up), w1)
        incoming = lax.ppermute(grad_in, "segment", [(plane, plane - 1)])

    back, back_spreads, grad_pre = call(
        back_middle_kept,
        [CHUNK, Far(WIDE), Far(INNER)],
        *factors,
        scratch=[INNER],
        copies=3,
    )
    arrived = exchange(back)
    far = [Far(item) for item in (rows_last, rows, x, own[3], up, act, back_spreads)]
    far += [Far(mixed_in), Far(grad_pre)]
    shapes = [(COUNT, 512), own[3].shape, own[2].shape, own[1].shape]
    segment_outputs, fourth_grad, third_grad, second_grad = call(
        functools.partial(gradients, segments - 1),
        [Far(shape) for shape in shapes],
        here,
        *far,
        scratch=[WIDE, FLAT, own[3].shape, FLAT, INNER, WIDE, CHUNK, INNER] + shapes,
        copies=17,
        limit=2 * VMEM_BYTES,
    )
    grad_in, first_grad = call(
        back_leave, [(COUNT, 512), own[0].shape], arrived, up, own[0], x
    )
    return (
        segment_outputs[None],
        grad_in[None],
        first_grad[None],
        second_grad[None],
        third_grad[None],
        fourth_grad[None],
    )


def solution(mesh):
    placed = (
        P(None, "blk"),
        P(None, "blk"),
        P("segment", "blk", None, None),
        P("segment", "blk", None, None),
        P("segment", "blk", None, None),
        P("segment", "blk", None, None),
    )
    return jax.shard_map(
        shards,
        mesh=mesh,
        in_specs=placed,
        out_specs=(
            P("segment", None, "blk"),
            P("segment", None, "blk"),
            P("segment", "blk", None, None),
            P("segment", "blk", None, None),
            P("segment", "blk", None, None),
            P("segment", "blk", None, None),
        ),
        check_vma=False,
    )
```

```python
import functools

import jax
import jax.numpy as jnp
from jax import lax
from jax.experimental import pallas as pl
from jax.experimental.pallas import tpu as pltpu
from jax.sharding import PartitionSpec as P

VMEM_BYTES = 12 * 1024 * 1024
BF16 = jnp.bfloat16
F32 = jnp.float32
CUBIC = 0.044715
ROOT = 0.7978845608028654
COUNT = 256
PEERS = 32
FLAT = (512, COUNT)
CHUNK = (PEERS, 16, COUNT)
WIDE = (PEERS, 64, COUNT)
INNER = (2, 1024, COUNT)
PARTS = (2, 256, COUNT)


class Near:
    def __init__(self, value, kind=BF16):
        self.value = value
        self.kind = kind


class Far:
    def __init__(self, value):
        self.value = value


def call(body, outs, *args, scratch=(), copies=0, limit=VMEM_BYTES):
    place = pl.BlockSpec(memory_space=pltpu.VMEM)
    scalar = pl.BlockSpec(memory_space=pltpu.SMEM)
    far = pl.BlockSpec(memory_space=pltpu.HBM)
    specs, operands = [], []
    for arg in args:
        if isinstance(arg, Near):
            specs.append(place)
            operands.append(pltpu.with_memory_space_constraint(arg.value, pltpu.VMEM))
        elif isinstance(arg, Far):
            specs.append(far)
            operands.append(pltpu.with_memory_space_constraint(arg.value, pltpu.HBM))
        else:
            specs.append(scalar if arg.dtype == jnp.int32 else place)
            operands.append(arg)
    shapes, places = [], []
    for out in outs:
        if isinstance(out, Near):
            shapes.append(pltpu.VMEM(out.value, out.kind))
        elif isinstance(out, Far):
            shapes.append(pltpu.HBM(out.value, BF16))
        else:
            shapes.append(jax.ShapeDtypeStruct(out, BF16))
        places.append(far if isinstance(out, Far) else place)
    scratch_shapes = [pltpu.VMEM(shape, BF16) for shape in scratch]
    if copies:
        scratch_shapes.append(pltpu.SemaphoreType.DMA((copies,)))
    return pl.pallas_call(
        body,
        out_shape=shapes,
        in_specs=specs,
        out_specs=places,
        scratch_shapes=scratch_shapes,
        compiler_params=pltpu.CompilerParams(vmem_limit_bytes=limit),
    )(*operands)


class Copies:
    def __init__(self, done):
        self.done = done
        self.count = 0

    def start(self, source, target):
        copy = pltpu.make_async_copy(source, target, self.done.at[self.count])
        self.count += 1
        copy.start()
        return copy


def load_enter(tokens_far, *refs):
    sources, plain, turned = refs[0:4], refs[4:8], refs[8:12]
    x, mixed, tokens, done = refs[12:]
    copies = Copies(done)
    came = copies.start(tokens_far, tokens)
    ready = {}
    for i in (0, 2, 1, 3):
        ready[i] = [copies.start(sources[i].at[b], plain[i].at[b]) for b in range(2)]
    came.wait()
    x[...] = tokens[...].T
    for i in (0, 2, 1, 3):
        for b in range(2):
            ready[i][b].wait()
            turned[i][b] = plain[i][b].T
        if i == 0:
            mixed[...] = interleave(
                *[dot(turned[0][k], x[256 * k : 256 * (k + 1), :]) for k in range(2)]
            )


def dot(left, right):
    return lax.dot_general(left, right, (((1,), (0,)), ((), ())), preferred_element_type=F32)


def dot_nt(left, right):
    return lax.dot_general(left, right, (((1,), (1,)), ((), ())), preferred_element_type=F32)


def upper_rows(shape):
    return lax.rem(lax.broadcasted_iota(jnp.int32, shape, 0), 8) < 4


def interleave(a, b):
    upper = upper_rows(a.shape)
    first = jnp.where(upper, a, pltpu.roll(b, 4, 0))
    second = jnp.where(upper, pltpu.roll(a, 252, 0), b)
    return stack_halves(first, second)


def stack_halves(first, second):
    tiles = [item.reshape(PEERS, 1, 8, COUNT) for item in (first, second)]
    return jnp.concatenate(tiles, axis=1).reshape(CHUNK).astype(BF16)


def halves_of(joined):
    tiles = joined.astype(F32).reshape(PEERS, 2, 8, COUNT)
    return [tiles[:, g].reshape(256, COUNT) for g in range(2)]


def separate(joined):
    first, second = halves_of(joined)
    upper = upper_rows(first.shape)
    a = jnp.where(upper, first, pltpu.roll(second, 4, 0))
    b = jnp.where(upper, pltpu.roll(first, 252, 0), second)
    return a.astype(BF16), b.astype(BF16)


def gelu_tanh(value):
    return jnp.tanh(ROOT * (value + CUBIC * (value * value * value)))


def gelu(value):
    return 0.5 * value * (1.0 + gelu_tanh(value))


def gelu_slope(value, bend):
    slope = ROOT * (1.0 + 3.0 * CUBIC * (value * value))
    return 0.5 * (1.0 + bend) + (0.5 * value * (1.0 - bend * bend)) * slope


def middle(arrived, w2_up, w3_up, spread, act):
    joined = [half.astype(BF16) for half in halves_of(arrived[...])]
    for g in range(2):
        for start in range(0, 1024, 256):
            rows = slice(start, start + 256)
            pre = dot(w2_up[g, rows, :], joined[g]).astype(BF16)
            act[g, rows, :] = gelu(pre.astype(F32)).astype(BF16)
    for g in range(2):
        spread_rows(w3_up, act, spread, g)


def spread_rows(w3_up, act, spread, g):
    for start in range(0, 1024, 256):
        out = dot(w3_up[g, start : start + 256, :], act[g]).astype(BF16)
        peers = slice(start // 32, start // 32 + 8)
        spread[peers, 32 * g : 32 * (g + 1), :] = out.reshape(8, 32, COUNT)


def middle_kept(arrived, w2_up, w3_up, spread, slope, mixed_far, act_far, act, done):
    copies = Copies(done)
    leaving = [copies.start(arrived, mixed_far)]
    joined = [half.astype(BF16) for half in halves_of(arrived[...])]
    for g in range(2):
        for start in range(0, 1024, 256):
            rows = slice(start, start + 256)
            pre = dot(w2_up[g, rows, :], joined[g]).astype(BF16).astype(F32)
            bend = gelu_tanh(pre)
            act[g, rows, :] = (0.5 * pre * (1.0 + bend)).astype(BF16)
            slope[g, rows, :] = gelu_slope(pre, bend)
        leaving.append(copies.start(act.at[g], act_far.at[g]))
    for g in range(2):
        spread_rows(w3_up, act, spread, g)
    for copy in leaving:
        copy.wait()


def middle_or_first(plane, here, arrived, w2_up, w3_up, far_tokens, w4, spread, up, tokens, act, done):
    @pl.when(here[0] == plane)
    def _():
        Copies(done).start(far_tokens, tokens).wait()
        up[...] = tokens[...].T
        back_spread(up, w4, spread)

    @pl.when(here[0] != plane)
    def _():
        up[...] = jnp.zeros_like(up)
        middle(arrived, w2_up, w3_up, spread, act)


def leave_rows(arrived, w4_up, x, out):
    rows = arrived[...].reshape(64, 32, COUNT)
    for k in range(2):
        part = rows[:, 16 * k : 16 * (k + 1), :].reshape(1024, COUNT)
        place = slice(256 * k, 256 * (k + 1))
        out[place, :] = (x[place, :].astype(F32) + dot(w4_up[k], part)).astype(BF16)


def leave(arrived, x, w4_up, out):
    leave_rows(arrived, w4_up, x, out)


def enter_choice(plane, here, incoming, held, w1_up, x, mixed):
    x[...] = jnp.where(here[0] == plane, incoming[...], held[...])
    mixed[...] = interleave(*[dot(w1_up[k], x[256 * k : 256 * (k + 1), :]) for k in range(2)])


def back_spread(up, w4, spread):
    parts = []
    for k in range(2):
        part = dot(w4[k], up[256 * k : 256 * (k + 1), :]).astype(BF16)
        parts.append(part.reshape(64, 1, 16, COUNT))
    spread[...] = jnp.concatenate(parts, axis=1).reshape(WIDE)


def unmix(joined, w1, up, out):
    for k, part in enumerate(separate(joined)):
        rows = slice(256 * k, 256 * (k + 1))
        out[rows, :] = (up[rows, :].astype(F32) + dot(w1[k], part)).astype(BF16)


def back_enter_choice(plane, here, incoming, held, w4, up, spread):
    up[...] = jnp.where(here[0] == plane, incoming[...], held[...])
    back_spread(up, w4, spread)


def back_enter_or_last(plane, here, ready, incoming, held, w4, up, spread):
    @pl.when(here[0] == plane + 1)
    def _():
        up[...] = held[...]
        spread[...] = ready[...]

    @pl.when(here[0] != plane + 1)
    def _():
        back_enter_choice(plane, here, incoming, held, w4, up, spread)


def back_step(arrived, up, w1, out):
    unmix(arrived[...], w1, up, out)


def back_product(arrived, slope, w3, g, grad_pre):
    part = arrived[:, 32 * g : 32 * (g + 1), :].reshape(1024, COUNT)
    for start in range(0, 1024, 256):
        rows = slice(start, start + 256)
        grad_pre[g, rows, :] = (dot(w3[g, rows, :], part) * slope[g, rows, :]).astype(BF16)


def back_middle(arrived, slope, w2, w3, back, grad_pre):
    for g in range(2):
        back_product(arrived, slope, w3, g, grad_pre)
    back[...] = stack_halves(*[dot(w2[g], grad_pre[g]) for g in range(2)])


def back_middle_kept(arrived, slope, w2, w3, back, arrived_far, pre_far, grad_pre, done):
    copies = Copies(done)
    leaving = [copies.start(arrived, arrived_far)]
    for g in range(2):
        back_product(arrived, slope, w3, g, grad_pre)
        leaving.append(copies.start(grad_pre.at[g], pre_far.at[g]))
    back[...] = stack_halves(*[dot(w2[g], grad_pre[g]) for g in range(2)])
    for copy in leaving:
        copy.wait()


def gradients(plane, here, *refs):
    new_in, held_in, x_in, w4_in, up_in, act_in, back_in, mixed_in, pre_in = refs[0:9]
    out_far, fourth_far, third_far, second_far = refs[9:13]
    rows, x, w4, up, act, back, mixed, pre, out, fourth, third, second, done = refs[13:]
    copies = Copies(done)
    act_ready = copies.start(act_in, act)
    back_ready = copies.start(back_in, back)
    ready = [copies.start(mixed_in, mixed), copies.start(pre_in, pre)]
    ready += [copies.start(x_in, x), copies.start(up_in, up), copies.start(w4_in, w4)]
    rows_done = done.at[copies.count]
    copies.count += 1

    @pl.when(here[0] == plane)
    def _():
        pltpu.make_async_copy(new_in, rows, rows_done).start()

    @pl.when(here[0] != plane)
    def _():
        pltpu.make_async_copy(held_in, rows, rows_done).start()

    leaving = []
    act_ready.wait()
    back_ready.wait()
    for g in range(2):
        part = back[:, 32 * g : 32 * (g + 1), :].reshape(1024, COUNT)
        for half in range(2):
            band = pl.ds(512 * half, 512)
            for start in (512 * half, 512 * half + 256):
                place = slice(start, start + 256)
                third[g, place, :] = dot_nt(act[g, place, :], part).astype(BF16)
            leaving.append(copies.start(third.at[g, band], third_far.at[g, band]))
    for copy in ready:
        copy.wait()
    for g, part in enumerate(halves_of(mixed[...])):
        second[g] = dot_nt(part.astype(BF16), pre[g]).astype(BF16)
        leaving.append(copies.start(second.at[g], second_far.at[g]))
    pltpu.make_async_copy(held_in, rows, rows_done).wait()
    joined = rows[...].reshape(64, 32, COUNT)
    for k in range(2):
        part = joined[:, 16 * k : 16 * (k + 1), :].reshape(1024, COUNT)
        place = slice(256 * k, 256 * (k + 1))
        fourth[k] = dot_nt(part, up[place, :]).astype(BF16)
        leaving.append(copies.start(fourth.at[k], fourth_far.at[k]))
        total = x[place, :].astype(F32) + dot(w4[k].T, part)
        out[:, place] = total.astype(BF16).T
    leaving.append(copies.start(out, out_far))
    for copy in leaving:
        copy.wait()


def back_leave(arrived, up, w1, x, out, grad):
    for k, part in enumerate(separate(arrived[...])):
        place = slice(256 * k, 256 * (k + 1))
        total = up[place, :].astype(F32) + dot(w1[k], part)
        out[:, place] = total.astype(BF16).T
        grad[k] = dot_nt(x[place, :], part).astype(BF16)


def exchange(block):
    return lax.all_to_all(block, "blk", split_axis=0, concat_axis=0, tiled=True)


def shards(tokens, cotangent, first_factor, second_factor, third_factor, fourth_factor):
    segments = lax.axis_size("segment")
    position = lax.axis_index("segment")
    own = (first_factor[0], second_factor[0], third_factor[0], fourth_factor[0])

    here = position.astype(jnp.int32).reshape(1)
    tokens, here = lax.optimization_barrier((tokens, here))
    flipped = [(w.shape[0], w.shape[2], w.shape[1]) for w in own]
    results = call(
        load_enter,
        [Near(w.shape) for w in own] + [Near(f) for f in flipped] + [Near(FLAT), Near(CHUNK)],
        Far(tokens),
        *[Far(w) for w in own],
        scratch=[(COUNT, 512)],
        copies=9,
    )
    w1, w2, w3, w4, w1_up, w2_up, w3_up, w4_up = [Near(item) for item in results[:8]]
    x, mixed = results[8:]

    for step in range(segments):
        if step:
            x, mixed = call(
                functools.partial(enter_choice, step),
                [Near(FLAT), Near(CHUNK)],
                here,
                Near(incoming),
                Near(x),
                w1_up,
            )
        arrived = exchange(mixed)
        if step < segments - 2:
            (spread,) = call(
                middle, [Near(WIDE)], Near(arrived), w2_up, w3_up, scratch=[INNER]
            )
        elif step == segments - 2:
            spread, up = call(
                functools.partial(middle_or_first, segments - 1),
                [Near(WIDE), Near(FLAT)],
                here,
                Near(arrived),
                w2_up,
                w3_up,
                Far(cotangent),
                w4,
                scratch=[(COUNT, 512), INNER],
                copies=1,
            )
        else:
            spread, slope, mixed_in, act = call(
                middle_kept,
                [Near(WIDE), Near(INNER, F32), Far(CHUNK), Far(INNER)],
                Near(arrived),
                w2_up,
                w3_up,
                scratch=[INNER],
                copies=3,
            )
            break
        rows = exchange(spread)
        (out,) = call(leave, [Near(FLAT)], Near(rows), Near(x), w4_up)
        incoming = lax.ppermute(out, "segment", [(step, step + 1)])

    gathered = rows
    for step in range(segments):
        last = step == segments - 1
        plane = segments - 1 - step
        if step == 1:
            up, spread = call(
                functools.partial(back_enter_or_last, plane),
                [Near(FLAT), Near(WIDE)],
                here,
                Near(spread),
                Near(incoming),
                Near(up),
                w4,
            )
            rows_last = gathered = exchange(spread)
        elif step:
            up, spread = call(
                functools.partial(back_enter_choice, plane),
                [Near(FLAT), Near(WIDE)],
                here,
                Near(incoming),
                Near(up),
                w4,
            )
            gathered = exchange(spread)
        factors = (Near(gathered), Near(slope), w2, w3)
        if last:
            break
        (back,) = call(back_middle, [Near(CHUNK)], *factors, scratch=[INNER])
        arrived = exchange(back)
        (grad_in,) = call(back_step, [Near(FLAT)], Near(arrived), Near(up), w1)
        incoming = lax.ppermute(grad_in, "segment", [(plane, plane - 1)])

    back, back_spreads, grad_pre = call(
        back_middle_kept,
        [CHUNK, Far(WIDE), Far(INNER)],
        *factors,
        scratch=[INNER],
        copies=3,
    )
    arrived = exchange(back)
    far = [Far(item) for item in (rows_last, rows, x, own[3], up, act, back_spreads)]
    far += [Far(mixed_in), Far(grad_pre)]
    shapes = [(COUNT, 512), own[3].shape, own[2].shape, own[1].shape]
    segment_outputs, fourth_grad, third_grad, second_grad = call(
        functools.partial(gradients, segments - 1),
        [Far(shape) for shape in shapes],
        here,
        *far,
        scratch=[WIDE, FLAT, own[3].shape, FLAT, INNER, WIDE, CHUNK, INNER] + shapes,
        copies=17,
        limit=2 * VMEM_BYTES,
    )
    grad_in, first_grad = call(
        back_leave, [(COUNT, 512), own[0].shape], arrived, up, own[0], x
    )
    return (
        segment_outputs[None],
        grad_in[None],
        first_grad[None],
        second_grad[None],
        third_grad[None],
        fourth_grad[None],
    )


def solution(mesh):
    placed = (
        P(None, "blk"),
        P(None, "blk"),
        P("segment", "blk", None, None),
        P("segment", "blk", None, None),
        P("segment", "blk", None, None),
        P("segment", "blk", None, None),
    )
    return jax.shard_map(
        shards,
        mesh=mesh,
        in_specs=placed,
        out_specs=(
            P("segment", None, "blk"),
            P("segment", None, "blk"),
            P("segment", "blk", None, None),
            P("segment", "blk", None, None),
            P("segment", "blk", None, None),
            P("segment", "blk", None, None),
        ),
        check_vma=False,
    )
```

```python
import functools

import jax
import jax.numpy as jnp
from jax import lax
from jax.experimental import pallas as pl
from jax.experimental.pallas import tpu as pltpu
from jax.sharding import PartitionSpec as P

VMEM_BYTES = 12 * 1024 * 1024
BF16 = jnp.bfloat16
F32 = jnp.float32
CUBIC = 0.044715
ROOT = 0.7978845608028654
COUNT = 256
PEERS = 32
FLAT = (512, COUNT)
CHUNK = (PEERS, 16, COUNT)
WIDE = (PEERS, 64, COUNT)
INNER = (2, 1024, COUNT)
PARTS = (2, 256, COUNT)


class Near:
    def __init__(self, value, kind=BF16):
        self.value = value
        self.kind = kind


class Far:
    def __init__(self, value):
        self.value = value


def call(body, outs, *args, scratch=(), copies=0, limit=VMEM_BYTES):
    place = pl.BlockSpec(memory_space=pltpu.VMEM)
    scalar = pl.BlockSpec(memory_space=pltpu.SMEM)
    far = pl.BlockSpec(memory_space=pltpu.HBM)
    specs, operands = [], []
    for arg in args:
        if isinstance(arg, Near):
            specs.append(place)
            operands.append(pltpu.with_memory_space_constraint(arg.value, pltpu.VMEM))
        elif isinstance(arg, Far):
            specs.append(far)
            operands.append(pltpu.with_memory_space_constraint(arg.value, pltpu.HBM))
        else:
            specs.append(scalar if arg.dtype == jnp.int32 else place)
            operands.append(arg)
    shapes, places = [], []
    for out in outs:
        if isinstance(out, Near):
            shapes.append(pltpu.VMEM(out.value, out.kind))
        elif isinstance(out, Far):
            shapes.append(pltpu.HBM(out.value, BF16))
        else:
            shapes.append(jax.ShapeDtypeStruct(out, BF16))
        places.append(far if isinstance(out, Far) else place)
    scratch_shapes = [pltpu.VMEM(shape, BF16) for shape in scratch]
    if copies:
        scratch_shapes.append(pltpu.SemaphoreType.DMA((copies,)))
    return pl.pallas_call(
        body,
        out_shape=shapes,
        in_specs=specs,
        out_specs=places,
        scratch_shapes=scratch_shapes,
        compiler_params=pltpu.CompilerParams(vmem_limit_bytes=limit),
    )(*operands)


class Copies:
    def __init__(self, done):
        self.done = done
        self.count = 0

    def start(self, source, target):
        copy = pltpu.make_async_copy(source, target, self.done.at[self.count])
        self.count += 1
        copy.start()
        return copy


def load_enter(tokens_far, *refs):
    sources, plain, turned = refs[0:4], refs[4:8], refs[8:12]
    x, mixed, tokens, done = refs[12:]
    copies = Copies(done)
    came = copies.start(tokens_far, tokens)
    ready = {}
    for i in (0, 2, 1, 3):
        ready[i] = [copies.start(sources[i].at[b], plain[i].at[b]) for b in range(2)]
    came.wait()
    x[...] = tokens[...].T
    for i in (0, 2, 1, 3):
        for b in range(2):
            ready[i][b].wait()
            turned[i][b] = plain[i][b].T
        if i == 0:
            mixed[...] = interleave(
                *[dot(turned[0][k], x[256 * k : 256 * (k + 1), :]) for k in range(2)]
            )


def dot(left, right):
    return lax.dot_general(left, right, (((1,), (0,)), ((), ())), preferred_element_type=F32)


def dot_nt(left, right):
    return lax.dot_general(left, right, (((1,), (1,)), ((), ())), preferred_element_type=F32)


def upper_rows(shape):
    return lax.rem(lax.broadcasted_iota(jnp.int32, shape, 0), 8) < 4


def interleave(a, b):
    upper = upper_rows(a.shape)
    first = jnp.where(upper, a, pltpu.roll(b, 4, 0))
    second = jnp.where(upper, pltpu.roll(a, 252, 0), b)
    return stack_halves(first, second)


def stack_halves(first, second):
    tiles = [item.reshape(PEERS, 1, 8, COUNT) for item in (first, second)]
    return jnp.concatenate(tiles, axis=1).reshape(CHUNK).astype(BF16)


def halves_of(joined):
    tiles = joined.astype(F32).reshape(PEERS, 2, 8, COUNT)
    return [tiles[:, g].reshape(256, COUNT) for g in range(2)]


def separate(joined):
    first, second = halves_of(joined)
    upper = upper_rows(first.shape)
    a = jnp.where(upper, first, pltpu.roll(second, 4, 0))
    b = jnp.where(upper, pltpu.roll(first, 252, 0), second)
    return a.astype(BF16), b.astype(BF16)


def gelu_tanh(value):
    return jnp.tanh(ROOT * (value + CUBIC * (value * value * value)))


def gelu(value):
    return 0.5 * value * (1.0 + gelu_tanh(value))


def gelu_slope(value, bend):
    slope = ROOT * (1.0 + 3.0 * CUBIC * (value * value))
    return 0.5 * (1.0 + bend) + (0.5 * value * (1.0 - bend * bend)) * slope


def middle(arrived, w2_up, w3_up, spread, act):
    joined = [half.astype(BF16) for half in halves_of(arrived[...])]
    for g in range(2):
        for start in range(0, 1024, 256):
            rows = slice(start, start + 256)
            pre = dot(w2_up[g, rows, :], joined[g]).astype(BF16)
            act[g, rows, :] = gelu(pre.astype(F32)).astype(BF16)
    for g in range(2):
        spread_rows(w3_up, act, spread, g)


def spread_rows(w3_up, act, spread, g):
    for start in range(0, 1024, 256):
        out = dot(w3_up[g, start : start + 256, :], act[g]).astype(BF16)
        peers = slice(start // 32, start // 32 + 8)
        spread[peers, 32 * g : 32 * (g + 1), :] = out.reshape(8, 32, COUNT)


def turn(arrived, gathered, w2_up, w3_up, w2, w3, *refs):
    spread, slope, mixed_far, act_far, back, act, grad_pre, done = refs
    copies = Copies(done)
    leaving = [copies.start(arrived, mixed_far)]
    joined = [half.astype(BF16) for half in halves_of(arrived[...])]
    for g in range(2):
        for start in range(0, 1024, 256):
            rows = slice(start, start + 256)
            pre = dot(w2_up[g, rows, :], joined[g]).astype(BF16).astype(F32)
            bend = gelu_tanh(pre)
            act[g, rows, :] = (0.5 * pre * (1.0 + bend)).astype(BF16)
            slope[g, rows, :] = gelu_slope(pre, bend)
        leaving.append(copies.start(act.at[g], act_far.at[g]))
    for g in range(2):
        spread_rows(w3_up, act, spread, g)
    back_middle(gathered, slope, w2, w3, back, grad_pre)
    for copy in leaving:
        copy.wait()


def middle_or_first(plane, here, arrived, w2_up, w3_up, far_tokens, w4, spread, up, tokens, act, done):
    @pl.when(here[0] == plane)
    def _():
        Copies(done).start(far_tokens, tokens).wait()
        up[...] = tokens[...].T
        back_spread(up, w4, spread)

    @pl.when(here[0] != plane)
    def _():
        up[...] = jnp.zeros_like(up)
        middle(arrived, w2_up, w3_up, spread, act)


def leave_rows(arrived, w4_up, x, out):
    rows = arrived[...].reshape(64, 32, COUNT)
    for k in range(2):
        part = rows[:, 16 * k : 16 * (k + 1), :].reshape(1024, COUNT)
        place = slice(256 * k, 256 * (k + 1))
        out[place, :] = (x[place, :].astype(F32) + dot(w4_up[k], part)).astype(BF16)


def leave(arrived, x, w4_up, out):
    leave_rows(arrived, w4_up, x, out)


def enter_choice(plane, here, incoming, held, w1_up, x, mixed):
    x[...] = jnp.where(here[0] == plane, incoming[...], held[...])
    mixed[...] = interleave(*[dot(w1_up[k], x[256 * k : 256 * (k + 1), :]) for k in range(2)])


def back_spread(up, w4, spread):
    parts = []
    for k in range(2):
        part = dot(w4[k], up[256 * k : 256 * (k + 1), :]).astype(BF16)
        parts.append(part.reshape(64, 1, 16, COUNT))
    spread[...] = jnp.concatenate(parts, axis=1).reshape(WIDE)


def unmix(joined, w1, up, out):
    for k, part in enumerate(separate(joined)):
        rows = slice(256 * k, 256 * (k + 1))
        out[rows, :] = (up[rows, :].astype(F32) + dot(w1[k], part)).astype(BF16)


def back_enter_choice(plane, here, incoming, held, w4, up, spread):
    up[...] = jnp.where(here[0] == plane, incoming[...], held[...])
    back_spread(up, w4, spread)


def back_enter_or_last(plane, here, ready, incoming, held, w4, up, spread):
    @pl.when(here[0] == plane + 1)
    def _():
        up[...] = held[...]
        spread[...] = ready[...]

    @pl.when(here[0] != plane + 1)
    def _():
        back_enter_choice(plane, here, incoming, held, w4, up, spread)


def back_step(arrived, up, w1, out):
    unmix(arrived[...], w1, up, out)


def back_product(arrived, slope, w3, g, grad_pre):
    part = arrived[:, 32 * g : 32 * (g + 1), :].reshape(1024, COUNT)
    for start in range(0, 1024, 256):
        rows = slice(start, start + 256)
        grad_pre[g, rows, :] = (dot(w3[g, rows, :], part) * slope[g, rows, :]).astype(BF16)


def back_middle(arrived, slope, w2, w3, back, grad_pre):
    for g in range(2):
        back_product(arrived, slope, w3, g, grad_pre)
    back[...] = stack_halves(*[dot(w2[g], grad_pre[g]) for g in range(2)])


def back_middle_kept(arrived, slope, w2, w3, back, arrived_far, pre_far, grad_pre, done):
    copies = Copies(done)
    leaving = [copies.start(arrived, arrived_far)]
    for g in range(2):
        back_product(arrived, slope, w3, g, grad_pre)
        leaving.append(copies.start(grad_pre.at[g], pre_far.at[g]))
    back[...] = stack_halves(*[dot(w2[g], grad_pre[g]) for g in range(2)])
    for copy in leaving:
        copy.wait()


def gradients(plane, here, *refs):
    new_in, held_in, x_in, w4_in, up_in, act_in, back_in, mixed_in, pre_in = refs[0:9]
    out_far, fourth_far, third_far, second_far = refs[9:13]
    rows, x, w4, up, act, back, mixed, pre, out, fourth, third, second, done = refs[13:]
    copies = Copies(done)
    act_ready = copies.start(act_in, act)
    back_ready = copies.start(back_in, back)
    ready = [copies.start(mixed_in, mixed), copies.start(pre_in, pre)]
    ready += [copies.start(x_in, x), copies.start(up_in, up), copies.start(w4_in, w4)]
    rows_done = done.at[copies.count]
    copies.count += 1

    @pl.when(here[0] == plane)
    def _():
        pltpu.make_async_copy(new_in, rows, rows_done).start()

    @pl.when(here[0] != plane)
    def _():
        pltpu.make_async_copy(held_in, rows, rows_done).start()

    leaving = []
    act_ready.wait()
    back_ready.wait()
    for g in range(2):
        part = back[:, 32 * g : 32 * (g + 1), :].reshape(1024, COUNT)
        for half in range(2):
            band = pl.ds(512 * half, 512)
            for start in (512 * half, 512 * half + 256):
                place = slice(start, start + 256)
                third[g, place, :] = dot_nt(act[g, place, :], part).astype(BF16)
            leaving.append(copies.start(third.at[g, band], third_far.at[g, band]))
    for copy in ready:
        copy.wait()
    for g, part in enumerate(halves_of(mixed[...])):
        second[g] = dot_nt(part.astype(BF16), pre[g]).astype(BF16)
        leaving.append(copies.start(second.at[g], second_far.at[g]))
    pltpu.make_async_copy(held_in, rows, rows_done).wait()
    joined = rows[...].reshape(64, 32, COUNT)
    for k in range(2):
        part = joined[:, 16 * k : 16 * (k + 1), :].reshape(1024, COUNT)
        place = slice(256 * k, 256 * (k + 1))
        fourth[k] = dot_nt(part, up[place, :]).astype(BF16)
        leaving.append(copies.start(fourth.at[k], fourth_far.at[k]))
        total = x[place, :].astype(F32) + dot(w4[k].T, part)
        out[:, place] = total.astype(BF16).T
    leaving.append(copies.start(out, out_far))
    for copy in leaving:
        copy.wait()


def back_leave(arrived, up, w1, x, out, grad):
    for k, part in enumerate(separate(arrived[...])):
        place = slice(256 * k, 256 * (k + 1))
        total = up[place, :].astype(F32) + dot(w1[k], part)
        out[:, place] = total.astype(BF16).T
        grad[k] = dot_nt(x[place, :], part).astype(BF16)


def exchange(block):
    return lax.all_to_all(block, "blk", split_axis=0, concat_axis=0, tiled=True)


def shards(tokens, cotangent, first_factor, second_factor, third_factor, fourth_factor):
    segments = lax.axis_size("segment")
    position = lax.axis_index("segment")
    own = (first_factor[0], second_factor[0], third_factor[0], fourth_factor[0])

    here = position.astype(jnp.int32).reshape(1)
    tokens, here = lax.optimization_barrier((tokens, here))
    flipped = [(w.shape[0], w.shape[2], w.shape[1]) for w in own]
    results = call(
        load_enter,
        [Near(w.shape) for w in own] + [Near(f) for f in flipped] + [Near(FLAT), Near(CHUNK)],
        Far(tokens),
        *[Far(w) for w in own],
        scratch=[(COUNT, 512)],
        copies=9,
    )
    w1, w2, w3, w4, w1_up, w2_up, w3_up, w4_up = [Near(item) for item in results[:8]]
    x, mixed = results[8:]

    for step in range(segments):
        if step:
            x, mixed = call(
                functools.partial(enter_choice, step),
                [Near(FLAT), Near(CHUNK)],
                here,
                Near(incoming),
                Near(x),
                w1_up,
            )
        arrived = exchange(mixed)
        if step < segments - 2:
            (spread,) = call(
                middle, [Near(WIDE)], Near(arrived), w2_up, w3_up, scratch=[INNER]
            )
        elif step == segments - 2:
            spread, up = call(
                functools.partial(middle_or_first, segments - 1),
                [Near(WIDE), Near(FLAT)],
                here,
                Near(arrived),
                w2_up,
                w3_up,
                Far(cotangent),
                w4,
                scratch=[(COUNT, 512), INNER],
                copies=1,
            )
        else:
            spread, slope, mixed_in, act, back = call(
                turn,
                [Near(WIDE), Near(INNER, F32), Far(CHUNK), Far(INNER), Near(CHUNK)],
                Near(arrived),
                Near(rows),
                w2_up,
                w3_up,
                w2,
                w3,
                scratch=[INNER, INNER],
                copies=3,
            )
            break
        rows = exchange(spread)
        (out,) = call(leave, [Near(FLAT)], Near(rows), Near(x), w4_up)
        incoming = lax.ppermute(out, "segment", [(step, step + 1)])

    for step in range(segments):
        last = step == segments - 1
        plane = segments - 1 - step
        if step == 1:
            up, spread = call(
                functools.partial(back_enter_or_last, plane),
                [Near(FLAT), Near(WIDE)],
                here,
                Near(spread),
                Near(incoming),
                Near(up),
                w4,
            )
            rows_last = gathered = exchange(spread)
        elif step:
            up, spread = call(
                functools.partial(back_enter_choice, plane),
                [Near(FLAT), Near(WIDE)],
                here,
                Near(incoming),
                Near(up),
                w4,
            )
            gathered = exchange(spread)
        if step:
            factors = (Near(gathered), Near(slope), w2, w3)
            if last:
                break
            (back,) = call(back_middle, [Near(CHUNK)], *factors, scratch=[INNER])
        arrived = exchange(back)
        (grad_in,) = call(back_step, [Near(FLAT)], Near(arrived), Near(up), w1)
        incoming = lax.ppermute(grad_in, "segment", [(plane, plane - 1)])

    back, back_spreads, grad_pre = call(
        back_middle_kept,
        [CHUNK, Far(WIDE), Far(INNER)],
        *factors,
        scratch=[INNER],
        copies=3,
    )
    arrived = exchange(back)
    far = [Far(item) for item in (rows_last, rows, x, own[3], up, act, back_spreads)]
    far += [Far(mixed_in), Far(grad_pre)]
    shapes = [(COUNT, 512), own[3].shape, own[2].shape, own[1].shape]
    segment_outputs, fourth_grad, third_grad, second_grad = call(
        functools.partial(gradients, segments - 1),
        [Far(shape) for shape in shapes],
        here,
        *far,
        scratch=[WIDE, FLAT, own[3].shape, FLAT, INNER, WIDE, CHUNK, INNER] + shapes,
        copies=17,
        limit=2 * VMEM_BYTES,
    )
    grad_in, first_grad = call(
        back_leave, [(COUNT, 512), own[0].shape], arrived, up, own[0], x
    )
    return (
        segment_outputs[None],
        grad_in[None],
        first_grad[None],
        second_grad[None],
        third_grad[None],
        fourth_grad[None],
    )


def solution(mesh):
    placed = (
        P(None, "blk"),
        P(None, "blk"),
        P("segment", "blk", None, None),
        P("segment", "blk", None, None),
        P("segment", "blk", None, None),
        P("segment", "blk", None, None),
    )
    return jax.shard_map(
        shards,
        mesh=mesh,
        in_specs=placed,
        out_specs=(
            P("segment", None, "blk"),
            P("segment", None, "blk"),
            P("segment", "blk", None, None),
            P("segment", "blk", None, None),
            P("segment", "blk", None, None),
            P("segment", "blk", None, None),
        ),
        check_vma=False,
    )
```
